32 devices in a mesh: context: 8 (over z, x), channel: 4 (over y, core).
Axes of the slice: x: 2, y: 2, z: 4, core: 2. Of those that a mesh axis runs over, the one named last changes fastest.
Arguments:
- first_stream: bfloat16 [2048, 8192], P('context', 'channel'), may hold values from -6 to 6
- value_stream: bfloat16 [2048, 8192], P('context', 'channel'), may hold values from -6 to 6
- short_gate: bfloat16 [2048, 8192], P('context', 'channel'), may hold values from -6 to 6
- out_gate: bfloat16 [2048, 8192], P('context', 'channel'), may hold values from -250 to 250
- mr_filter: float32 [128, 8192], P(None, 'channel'), may hold values from -0.5 to 0.5
- li_residue: float32 [16, 8192], P(None, 'channel'), may hold values from -1.5 to 1.5
- li_rate: float32 [16, 8192], P(None, 'channel'), may hold values from 0.00014648438 to 0.05
- li_skip: float32 [8192], P('channel'), may hold values from 0.5 to 1.5
- norm_gain: float32 [8192], P('channel'), may hold values from 0.5 to 1.5
Outputs:
- mixed: bfloat16 [2048, 8192], P('context', 'channel')
The draws below stay inside these ranges and needn't reach their ends.
All inputs are finite; a program needn't handle non-finite values.
Results may differ from the reference program's by a relative error of at most 0.0064.
Values may be sent and summed in bfloat16 or wider, within the bound.
A program may use at most 64 MiB of HBM per device.

```python
import math
import jax
import jax.numpy as jnp
from jax import lax

D = 8192
TAPS = 128
POLES = 16
LENGTH = 2048
NFFT = 4096


def draw_out_gate(key, part):
    key_base = jax.random.fold_in(key, 11)
    key_col = jax.random.fold_in(key, 12)
    key_row = jax.random.fold_in(key, 13)
    columns = jnp.arange(D).astype(jnp.float32)
    col_scale = 10.0 ** (columns / D) * 2.0 ** jax.random.uniform(key_col, (D,), jnp.float32)
    row_scale = 10.0 ** jax.random.uniform(key_row, (LENGTH, 1), jnp.float32)
    base = jnp.clip(jax.random.normal(key_base, (LENGTH, D), jnp.float32), -5.0, 5.0)
    return (base * col_scale[None, :] * row_scale / 4.0).astype(jnp.bfloat16)


def block_scale(key, dims, shards, smallest, largest):
    def one(position, shards_of):
        steps = jax.random.uniform(jax.random.fold_in(jax.random.fold_in(key, 6), position), (shards_of,), jnp.float32, smallest / len(shards), largest / len(shards))
        return jnp.repeat(jnp.exp(steps), dims[position] // shards_of).reshape((-1,) + (1,) * (len(dims) - position - 1))

    level = one(*shards[0])
    for cut in shards[1:]:
        level = level * one(*cut)
    return level


def gaussian(key, extent, deviation, reach, split=(), kind=jnp.bfloat16):
    values = jax.random.normal(key, extent, jnp.float32) * deviation
    if len(split) > 0:
        values = block_scale(key, extent, split, -0.22, 0.18) * values
    return jnp.clip(values, min=-reach, max=reach).astype(kind)


def setup_inputs(seed: int = 0) -> dict:
    arg_keys = jax.random.split(jax.random.key(seed), 10)
    first_stream = gaussian(arg_keys[0], (LENGTH, D), 1.0, 6.0, ((0, 8), (1, 4)))
    value_stream = gaussian(arg_keys[1], (LENGTH, D), 1.0, 6.0, ((0, 8), (1, 4)))
    short_gate = gaussian(arg_keys[2], (LENGTH, D), 1.0, 6.0, ((0, 8), (1, 4)))
    out_gate = draw_out_gate(jax.random.fold_in(arg_keys[9], 71), 0)
    mr_filter = gaussian(arg_keys[4], (TAPS, D), TAPS ** -0.5, 0.5, ((1, 4),), jnp.float32)
    li_residue = gaussian(arg_keys[5], (POLES, D), 0.25, 1.5, ((1, 4),), jnp.float32)
    li_rate = jnp.clip(jnp.exp(math.log(0.05) - 5.8328595 * jax.random.uniform(arg_keys[6], (POLES, D), jnp.float32) ** block_scale(arg_keys[6], (POLES, D), ((1, 4),), -0.2, 0.2)), 0.00014648438, 0.05)
    li_skip = jnp.clip(0.5 + 1.0 * jax.random.uniform(arg_keys[7], (D,), jnp.float32) ** block_scale(arg_keys[7], (D,), ((0, 4),), -0.2, 0.2), 0.5, 1.5)
    norm_gain = jnp.clip(1.0 + 0.1 * jax.random.normal(arg_keys[8], (D,), jnp.float32), 0.5, 1.5)
    return dict(first_stream=first_stream, value_stream=value_stream, short_gate=short_gate, out_gate=out_gate, mr_filter=mr_filter, li_residue=li_residue, li_rate=li_rate, li_skip=li_skip, norm_gain=norm_gain)


def column_block(array, index, width):
    return lax.dynamic_slice_in_dim(array, (index * width).astype(jnp.int32), width, array.ndim - 1)

def short_block(product, taps_block):
    signal = product.astype(jnp.float32)
    padded = jnp.concatenate([jnp.zeros((TAPS - 1, signal.shape[1]), jnp.float32), signal], 0)

    def add_tap(tap, total):
        start = (TAPS - 1 - tap).astype(jnp.int32)
        window = lax.dynamic_slice_in_dim(padded, start, LENGTH, 0)
        weight = lax.dynamic_slice_in_dim(taps_block, tap.astype(jnp.int32), 1, 0)
        return total + weight * window
    return lax.fori_loop(jnp.int32(0), jnp.int32(TAPS), add_tap, jnp.zeros((LENGTH, signal.shape[1]), jnp.float32))

def long_block(sequence, residue, rate):
    times = jnp.arange(LENGTH).astype(jnp.float32)
    impulse = jnp.zeros((LENGTH, sequence.shape[1]), jnp.float32)
    for index in range(POLES):
        impulse = impulse + residue[index][None, :] * jnp.sqrt(2.0 * rate[index][None, :]) * jnp.exp(-rate[index][None, :] * times[:, None])
    spectrum = jnp.fft.rfft(sequence.astype(jnp.float32), n=NFFT, axis=0) * jnp.fft.rfft(impulse, n=NFFT, axis=0)
    return jnp.fft.irfft(spectrum, n=NFFT, axis=0)[:LENGTH].astype(jnp.float32)

def reference(first_stream, value_stream, short_gate, out_gate, mr_filter, li_residue, li_rate, li_skip, norm_gain):
    width = 256
    blocks = D // width
    indices = jnp.arange(blocks).astype(jnp.int32)

    def first_pass(power_sum, index):
        first = column_block(first_stream, index, width).astype(jnp.float32)
        value = column_block(value_stream, index, width).astype(jnp.float32)
        product = (first * value).astype(jnp.bfloat16)
        short = short_block(product, column_block(mr_filter, index, width))
        mixed_short = (column_block(short_gate, index, width).astype(jnp.float32) * short).astype(jnp.bfloat16)
        long_conv = long_block(mixed_short, column_block(li_residue, index, width), column_block(li_rate, index, width))
        skip = column_block(li_skip, index, width)
        long_out = (long_conv + skip[None, :] * mixed_short.astype(jnp.float32)).astype(jnp.bfloat16)
        gated = column_block(out_gate, index, width).astype(jnp.float32) * long_out.astype(jnp.float32)
        return (power_sum + lax.optimization_barrier(jnp.sum(gated * gated, axis=1)), long_out)
    power_sum, long_blocks = lax.scan(first_pass, jnp.zeros((LENGTH,), jnp.float32), indices)
    scale = lax.rsqrt(power_sum / D + 1e-06)

    def second_pass(carry, pack):
        index, long_out = pack
        gated = column_block(out_gate, index, width).astype(jnp.float32) * long_out.astype(jnp.float32)
        gains = column_block(norm_gain, index, width)
        return (carry, (gated * scale[:, None] * gains[None, :]).astype(jnp.bfloat16))
    _, out_blocks = lax.scan(second_pass, jnp.zeros((), jnp.float32), (indices, long_blocks))
    return jnp.transpose(out_blocks, (1, 0, 2)).reshape(LENGTH, D)
```

```python
import functools

import jax
import jax.numpy as jnp
import numpy as np
from jax import lax
from jax.experimental import pallas as pl
from jax.experimental.pallas import tpu as pltpu
from jax.sharding import PartitionSpec as P

F32 = jnp.float32
BF16 = jnp.bfloat16
LANES = 128
SUB = 8


def split_const(a):
    hi = a.astype(BF16)
    lo = (a - hi.astype(np.float64)).astype(BF16)
    return hi, lo


def transforms(points, first, count, out_first, out_count, taps):
    freq = 2.0 * np.pi * (np.arange(points // 2) + 0.5) / points
    phase = freq[:, None] * np.arange(points)[None, :]
    full = np.concatenate([np.cos(phase), np.sin(phase)], 0)
    hi, lo = split_const(full[:, first : first + count])
    signal = np.concatenate([hi, lo], 1)
    hi, lo = split_const(full[:, :taps])
    taps_m = np.concatenate([hi, hi, lo], 1)
    hi, lo = split_const(full[:, out_first : out_first + out_count].T * (2.0 / points))
    back = np.concatenate([hi, hi, lo], 1)
    return signal, taps_m, back


def dot(a, b):
    return lax.dot_general(a, b, (((1,), (0,)), ((), ())), preferred_element_type=F32)


def three(v):
    hi = v.astype(BF16)
    lo = (v - hi.astype(F32)).astype(BF16)
    return jnp.concatenate([hi, lo, hi], 0)


def times_spectrum(x, h):
    half = x.shape[0] // 2
    xc, xs, hc, hs = x[:half], x[half:], h[:half], h[half:]
    return jnp.concatenate([xc * hc - xs * hs, xc * hs + xs * hc], 0)


def sublane_index():
    return lax.broadcasted_iota(jnp.int32, (SUB, LANES), 0).astype(F32)


def mode_sums(start, step, blocks, put):
    for a in range(blocks):
        total = start[0]
        for v in start[1:]:
            total = total + v
        put(a, total)
        if a + 1 < blocks:
            start = [v * e for v, e in zip(start, step)]


def rows_of(ref, lanes):
    return [ref[r : r + 1, lanes] for r in range(ref.shape[0])]


def spectra_kernel(filt, residue, rate, fs, fl, hs_out, hl_out, impulse):
    hs_out[...] = dot(fs[...], three(filt[...]))
    rows, width = impulse.shape
    sub = sublane_index()
    for tile in range(width // LANES):
        lanes = slice(tile * LANES, (tile + 1) * LANES)
        rates, res = rows_of(rate, lanes), rows_of(residue, lanes)
        start = [q * jnp.sqrt(2.0 * r) * jnp.exp(-r * sub) for q, r in zip(res, rates)]
        step = [jnp.broadcast_to(jnp.exp(-SUB * r), (SUB, LANES)) for r in rates]

        def put(a, v):
            impulse[a * SUB : (a + 1) * SUB, lanes] = v

        mode_sums(start, step, rows // SUB, put)
    hl_out[...] = dot(fl[...], three(impulse[...]))


def short_kernel(first, value, gate, halo, hs, rate, fs, gs, mixed_out, end_out):
    product = (first[...].astype(F32) * value[...].astype(F32)).astype(BF16)
    x = jnp.concatenate([halo[...], product], 0)
    y = times_spectrum(dot(fs[...], jnp.concatenate([x, x], 0)), hs[...])
    short = dot(gs[...], three(y))
    mixed_out[...] = (gate[...].astype(F32) * short).astype(BF16)
    rows, width = first.shape
    sub = sublane_index()
    for tile in range(width // LANES):
        lanes = slice(tile * LANES, (tile + 1) * LANES)
        rates = rows_of(rate, lanes)
        step = [jnp.broadcast_to(jnp.exp(-SUB * r), (SUB, LANES)) for r in rates]
        state = None
        for a in range(rows // 16):
            both = mixed_out[a * 16 : (a + 1) * 16, lanes].astype(F32)
            for part in (both[:SUB], both[SUB:]):
                state = [part] * len(step) if state is None else [s * e + part for s, e in zip(state, step)]
        for r, (s, q) in enumerate(zip(state, rates)):
            end_out[r : r + 1, lanes] = jnp.sum(s * jnp.exp(-q * (SUB - 1.0 - sub)), axis=0, keepdims=True)


def long_kernel(mixed, hl, skip, fl, gl, base_out):
    x = mixed[...]
    y = times_spectrum(dot(fl[...], jnp.concatenate([x, x], 0)), hl[...])
    base_out[...] = dot(gl[...], three(y)) + skip[...] * x.astype(F32)


def carry_kernel(base, carried, residue, rate, out_gate, long_out, power, total):
    rows, width = base.shape
    sub = sublane_index()
    for tile in range(width // LANES):
        lanes = slice(tile * LANES, (tile + 1) * LANES)
        rates, res, got = rows_of(rate, lanes), rows_of(residue, lanes), rows_of(carried, lanes)
        start = [g * q * jnp.sqrt(2.0 * r) * jnp.exp(-r * (sub + 1.0)) for g, q, r in zip(got, res, rates)]
        step = [jnp.broadcast_to(jnp.exp(-SUB * r), (SUB, LANES)) for r in rates]

        def put(a, v):
            total[a * SUB : (a + 1) * SUB, lanes] = v

        mode_sums(start, step, rows // SUB, put)
    out = (base[...] + total[...]).astype(BF16)
    long_out[...] = out
    gated = out_gate[...].astype(F32) * out.astype(F32)
    square = gated * gated
    fold = square[:, :LANES]
    for tile in range(1, width // LANES):
        fold = fold + square[:, tile * LANES : (tile + 1) * LANES]

    @pl.when(pl.program_id(0) == 0)
    def _():
        power[...] = fold

    @pl.when(pl.program_id(0) > 0)
    def _():
        power[...] += fold


def from_behind(value, axis, steps):
    count = lax.axis_size(axis)
    return lax.ppermute(value, axis, [(s, s + steps) for s in range(0, count - steps)])


def on_device(channels, first_stream, value_stream, short_gate, out_gate, mr_filter, li_residue, li_rate, li_skip, norm_gain):
    rows, width = first_stream.shape
    taps, poles = mr_filter.shape[0], li_residue.shape[0]
    chunk = min(256, width)
    grid = (width // chunk,)
    short_n, long_n = rows + taps, 2 * rows
    fs, fsh, gs = transforms(short_n, 0, short_n, taps, rows, taps)
    fl, flh, gl = transforms(long_n, 0, rows, 0, rows, rows)

    def col(n):
        return pl.BlockSpec((n, chunk), lambda i: (0, i))

    def whole(a):
        return pl.BlockSpec(a.shape, lambda i: (0, 0))

    params = pltpu.CompilerParams(vmem_limit_bytes=48 * 1024 * 1024)

    def cost(flops, size):
        return pl.CostEstimate(flops=int(flops), bytes_accessed=int(size), transcendentals=0)

    shape = jax.ShapeDtypeStruct
    tail = slice(rows - taps, rows)
    product_tail = (first_stream[tail].astype(F32) * value_stream[tail].astype(F32)).astype(BF16)
    halo = from_behind(product_tail, "context", 1)

    hs, hl = pl.pallas_call(
        spectra_kernel,
        grid=grid,
        in_specs=[col(taps), col(poles), col(poles), whole(fsh), whole(flh)],
        out_specs=[col(short_n), col(long_n)],
        out_shape=[shape((short_n, width), F32), shape((long_n, width), F32)],
        scratch_shapes=[pltpu.VMEM((rows, chunk), F32)],
        compiler_params=params,
        cost_estimate=cost(6e9, 8e6),
        name="spectra",
    )(mr_filter, li_residue, li_rate, fsh, flh)

    mixed, end_state = pl.pallas_call(
        short_kernel,
        grid=grid,
        in_specs=[col(rows), col(rows), col(rows), col(taps), col(short_n), col(poles), whole(fs), whole(gs)],
        out_specs=[col(rows), col(poles)],
        out_shape=[shape((rows, width), BF16), shape((poles, width), F32)],
        compiler_params=params,
        cost_estimate=cost(4e9, 8e6),
        name="short",
    )(first_stream, value_stream, short_gate, halo, hs, li_rate, fs, gs)

    count = lax.axis_size("context")
    sent = end_state.astype(BF16)
    near, far = from_behind(sent, "context", 1), from_behind(sent, "context", 2)
    state = near.astype(F32) + jnp.exp(-li_rate * rows) * far.astype(F32)
    span = 2
    while span < count:
        got = from_behind(state.astype(BF16), "context", span).astype(F32)
        state = state + jnp.exp(-li_rate * (rows * span)) * got
        span *= 2

    base = pl.pallas_call(
        long_kernel,
        grid=grid,
        in_specs=[col(rows), col(long_n), col(1), whole(fl), whole(gl)],
        out_specs=col(rows),
        out_shape=shape((rows, width), F32),
        compiler_params=params,
        cost_estimate=cost(4e9, 8e6),
        name="long",
    )(mixed, hl, li_skip[None, :], fl, gl)

    long_out, power = pl.pallas_call(
        carry_kernel,
        grid=grid,
        in_specs=[col(rows), col(poles), col(poles), col(poles), col(rows)],
        out_specs=[col(rows), pl.BlockSpec((rows, LANES), lambda i: (0, 0))],
        out_shape=[shape((rows, width), BF16), shape((rows, LANES), F32)],
        scratch_shapes=[pltpu.VMEM((rows, chunk), F32)],
        compiler_params=params,
        cost_estimate=cost(1e9, 5e6),
        name="carry",
    )(base, state, li_residue, li_rate, out_gate)

    scale = lax.rsqrt(lax.psum(jnp.sum(power, axis=1), "channel") / channels + 1e-06)
    gated = out_gate.astype(F32) * long_out.astype(F32)
    return (gated * scale[:, None] * norm_gain[None, :]).astype(BF16)


def solution(mesh):
    both, columns, channel = P("context", "channel"), P(None, "channel"), P("channel")

    def whole_arrays(*args):
        body = functools.partial(on_device, args[0].shape[1])
        return jax.shard_map(
            body,
            mesh=mesh,
            in_specs=(both,) * 4 + (columns,) * 3 + (channel,) * 2,
            out_specs=both,
            check_vma=False,
        )(*args)

    return whole_arrays
```

```python
import functools

import jax
import jax.numpy as jnp
import numpy as np
from jax import lax
from jax.experimental import pallas as pl
from jax.experimental.pallas import tpu as pltpu
from jax.sharding import PartitionSpec as P

F32 = jnp.float32
BF16 = jnp.bfloat16
LANES = 128
SUB = 8


def split_const(a):
    hi = a.astype(BF16)
    lo = (a - hi.astype(np.float64)).astype(BF16)
    return hi, lo


def transforms(points, out_first, out_count, taps):
    freq = 2.0 * np.pi * (np.arange(points // 2) + 0.5) / points
    phase = freq[:, None] * np.arange(points)[None, :]
    full = np.concatenate([np.cos(phase), np.sin(phase)], 0)
    hi, lo = split_const(full[:, :taps])
    taps_m = np.concatenate([hi, hi, lo], 1)
    hi, lo = split_const(full)
    both = np.concatenate([hi, lo], 1)
    back = full[:, out_first : out_first + out_count].T * (2.0 / points)
    return both, taps_m, back.astype(BF16)


def dot(a, b):
    return lax.dot_general(a, b, (((1,), (0,)), ((), ())), preferred_element_type=F32)


def three(v):
    hi = v.astype(BF16)
    lo = (v - hi.astype(F32)).astype(BF16)
    return jnp.concatenate([hi, lo, hi], 0)


def times_spectrum(x, h):
    half = x.shape[0] // 2
    xc, xs, hc, hs = x[:half], x[half:], h[:half], h[half:]
    return jnp.concatenate([xc * hc - xs * hs, xc * hs + xs * hc], 0)


def sublane_index():
    return lax.broadcasted_iota(jnp.int32, (SUB, LANES), 0).astype(F32)


def mode_sums(start, step, blocks, put):
    for a in range(blocks):
        total = start[0]
        for v in start[1:]:
            total = total + v
        put(a, total)
        if a + 1 < blocks:
            start = [v * e for v, e in zip(start, step)]


def rows_of(ref, lanes):
    return [ref[r : r + 1, lanes] for r in range(ref.shape[0])]


MESH = pl.DeviceIdType.MESH


def fused_kernel(n_ctx, n_chan, chunk, *refs):
    n_in = 14
    (first_h, value_h, gate_h, og_h, filt_h, res_h, rate_h, skip_h, fs_h, gs_h, fsh_h, flh_h, fl_h, gl_h) = refs[:n_in]
    long_out, power_out = refs[n_in : n_in + 2]
    (first, value, gate, og, filt, res, rate, skip, fs, gs, fsh, flh, fl, gl) = refs[n_in + 2 : 2 * n_in + 2]
    (x, hs, hl, impulse, mixed, base, total, end, sent, got, state, power, pow_row, pow_got, amp, step8, fade) = refs[
        2 * n_in + 2 : 2 * n_in + 19
    ]
    in_sem, halo_send, halo_recv, st_send, st_recv, pow_send, pow_recv = refs[2 * n_in + 19 :]

    rows, width = first.shape
    taps = filt.shape[0]
    chunks = width // chunk
    here, lane_group = lax.axis_index("context"), lax.axis_index("channel")
    head, tail = pl.ds(0, rows - taps), pl.ds(rows - taps, taps)

    pairs = [
        (first_h.at[tail], first.at[tail]),
        (value_h.at[tail], value.at[tail]),
        (filt_h, filt),
        (fsh_h, fsh),
        (res_h, res),
        (rate_h, rate),
        (flh_h, flh),
        (first_h.at[head], first.at[head]),
        (value_h.at[head], value.at[head]),
        (fs_h, fs),
        (gs_h, gs),
        (gate_h, gate),
        (skip_h, skip),
        (fl_h, fl),
        (gl_h, gl),
        (og_h, og),
    ]
    loads = [pltpu.make_async_copy(a, b, in_sem.at[i]) for i, (a, b) in enumerate(pairs)]
    for load in loads:
        load.start()

    spans = []
    while 2 << len(spans) < n_ctx:
        spans.append(2 << len(spans))
    offsets = sorted({k % n_ctx for s in [1, 2] + spans for k in (s, -s)} - {0})
    barrier = pltpu.get_barrier_semaphore()
    for k in offsets:
        pl.semaphore_signal(barrier, inc=1, device_id={"context": lax.rem(here + k, n_ctx)}, device_id_type=MESH)
    for k in range(1, n_chan):
        pl.semaphore_signal(barrier, inc=1, device_id={"channel": lax.rem(lane_group + k, n_chan)}, device_id_type=MESH)
    loads[0].wait()
    loads[1].wait()
    pl.semaphore_wait(barrier, len(offsets) + n_chan - 1)

    def at_chunk(c):
        return pl.ds(pl.multiple_of(c * chunk, chunk), chunk)

    def product(part, cols):
        return (first[part, cols].astype(F32) * value[part, cols].astype(F32)).astype(BF16)

    def halo_copy(c):
        cols = at_chunk(c)
        return pltpu.make_async_remote_copy(
            src_ref=x.at[pl.ds(rows, taps), cols],
            dst_ref=x.at[pl.ds(0, taps), cols],
            send_sem=halo_send.at[c],
            recv_sem=halo_recv.at[c],
            device_id={"context": lax.rem(here + 1, n_ctx)},
            device_id_type=MESH,
        )

    @pl.loop(0, chunks)
    def _(c):
        cols = at_chunk(c)
        x[pl.ds(rows, taps), cols] = product(tail, cols)
        halo_copy(c).start()

    for load in loads[2:7]:
        load.wait()
    amp[...] = res[...] * jnp.sqrt(2.0 * rate[...])
    step8[...] = jnp.exp(-SUB * rate[...])

    sub = sublane_index()
    poles = rate.shape[0]
    half = chunks // 2

    def lane_tiles(c):
        return [pl.ds(pl.multiple_of(c * chunk + t, LANES), LANES) for t in range(0, chunk, LANES)]

    def steps(lanes):
        return [jnp.broadcast_to(step8[r : r + 1, lanes], (SUB, LANES)) for r in range(poles)]

    def present(k):
        return jnp.where(here >= k, 1.0, 0.0).astype(F32)

    def spectra(c):
        cols = at_chunk(c)
        for t, lanes in enumerate(lane_tiles(c)):
            start = []
            for r in range(poles):
                fading = jnp.exp(-rate[r : r + 1, lanes] * sub)
                fade[r, :, lanes] = fading
                start.append(amp[r : r + 1, lanes] * fading)

            def put(a, v):
                impulse[a * SUB : (a + 1) * SUB, t * LANES : (t + 1) * LANES] = v

            mode_sums(start, steps(lanes), rows // SUB, put)
        hs[:, cols] = dot(fsh[...], three(filt[:, cols]))
        hl[:, cols] = dot(flh[...], three(impulse[...]))

    def short(c):
        cols = at_chunk(c)
        halo_copy(c).wait_recv()
        before = (x[pl.ds(0, taps), cols].astype(F32) * present(1)).astype(BF16)
        window = jnp.concatenate([before, product(head, cols), x[pl.ds(rows, taps), cols]], 0)
        y = times_spectrum(dot(fs[...], jnp.concatenate([window, window], 0)), hs[:, cols])
        out = dot(gs[...], y.astype(BF16))
        mixed[:, cols] = (gate[:, cols].astype(F32) * out).astype(BF16)

    def ends(c):
        for lanes in lane_tiles(c):
            step = steps(lanes)
            sums = None
            for a in range(0, rows, 16):
                both = mixed[a : a + 16, lanes].astype(F32)
                for part in (both[:SUB], both[SUB:]):
                    sums = [part] * poles if sums is None else [s * e + part for s, e in zip(sums, step)]
            for r, s in enumerate(sums):
                fading = jnp.exp(-rate[r : r + 1, lanes] * (SUB - 1.0 - sub))
                end[r : r + 1, lanes] = jnp.sum(s * fading, axis=0, keepdims=True)

    def local_long(c):
        cols = at_chunk(c)
        here_x = mixed[:, cols]
        y = times_spectrum(dot(fl[...], jnp.concatenate([here_x, here_x], 0)), hl[:, cols])
        base[:, cols] = dot(gl[...], y.astype(BF16)) + skip[:, cols] * here_x.astype(F32)

    def carry(c):
        for lanes in lane_tiles(c):
            start = [state[r : r + 1, lanes] * fade[r, :, lanes] for r in range(poles)]

            def put(a, v):
                total[a * SUB : (a + 1) * SUB, :] = v

            mode_sums(start, steps(lanes), rows // SUB, put)
            out = (base[:, lanes] + total[...]).astype(BF16)
            long_out[:, lanes] = out
            gated = og[:, lanes].astype(F32) * out.astype(F32)
            power[...] += gated * gated

    def scan(part):
        cols = pl.ds(part * half * chunk, half * chunk)

        def state_copy(slot, source, k):
            return pltpu.make_async_remote_copy(
                src_ref=sent.at[source, :, cols],
                dst_ref=got.at[slot, :, cols],
                send_sem=st_send.at[part, slot],
                recv_sem=st_recv.at[part, slot],
                device_id={"context": lax.rem(here + k, n_ctx)},
                device_id_type=MESH,
            )

        rates = rate[:, cols]
        sent[0, :, cols] = end[:, cols].astype(BF16)
        copies = [state_copy(0, 0, 1), state_copy(1, 0, 2)]
        for copy in copies:
            copy.start()
        yield
        for copy in copies:
            copy.wait_recv()
        now = got[0, :, cols].astype(F32) * present(1)
        now = now + jnp.exp(-rates * rows) * (got[1, :, cols].astype(F32) * present(2))
        for i, span in enumerate(spans):
            state[:, cols] = now
            sent[i + 1, :, cols] = now.astype(BF16)
            copy = state_copy(i + 2, i + 1, span)
            copy.start()
            copies.append(copy)
            yield
            copy.wait_recv()
            now = state[:, cols] + jnp.exp(-rates * (rows * span)) * (got[i + 2, :, cols].astype(F32) * present(span))
        state[:, cols] = now * amp[:, cols] * jnp.exp(-rates)
        for copy in copies:
            copy.wait_send()

    def run(body, first_chunk, last_chunk):
        if first_chunk < last_chunk:
            pl.loop(first_chunk, last_chunk)(body)

    def filter_and_next(c):
        short(c)
        spectra(c + 1)
        ends(c)

    spectra(0)
    for load in loads[7:12]:
        load.wait()
    run(filter_and_next, 0, half)
    early, late = scan(0), scan(1)
    next(early, None)
    run(filter_and_next, half, chunks - 1)
    next(early, None)
    short(chunks - 1)
    ends(chunks - 1)
    next(late, None)
    for load in loads[12:]:
        load.wait()
    run(local_long, 0, half)
    next(early, None)
    next(late, None)
    run(local_long, half, chunks)
    for _ in early:
        pass
    next(late, None)
    power[...] = jnp.zeros_like(power)
    run(carry, 0, half)
    for _ in late:
        pass
    run(carry, half, chunks)

    pow_row[...] = lax.dot_general(
        jnp.ones((SUB, LANES), F32),
        power[...],
        (((1,), (1,)), ((), ())),
        precision=lax.Precision.HIGHEST,
        preferred_element_type=F32,
    )
    shares = [
        pltpu.make_async_remote_copy(
            src_ref=pow_row,
            dst_ref=pow_got.at[k - 1],
            send_sem=pow_send.at[k - 1],
            recv_sem=pow_recv.at[k - 1],
            device_id={"channel": lax.rem(lane_group + k, n_chan)},
            device_id_type=MESH,
        )
        for k in range(1, n_chan)
    ]
    for copy in shares:
        copy.start()

    @pl.loop(0, chunks)
    def _(c):
        halo_copy(c).wait_send()

    for copy in shares:
        copy.wait()
    whole = pow_row[...]
    for k in range(n_chan - 1):
        whole = whole + pow_got[k]
    power_out[...] = whole


def on_device(channels, first_stream, value_stream, short_gate, out_gate, mr_filter, li_residue, li_rate, li_skip, norm_gain):
    rows, width = first_stream.shape
    taps, poles = mr_filter.shape[0], li_residue.shape[0]
    chunk = min(512, width // 2)
    chunks = width // chunk
    short_n, long_n = rows + taps, 2 * rows
    fs, fsh, gs = transforms(short_n, taps, rows, taps)
    fl, flh, gl = transforms(long_n, 0, rows, rows)
    fl = np.concatenate([fl[:, :rows], fl[:, long_n : long_n + rows]], 1)
    n_ctx, n_chan = lax.axis_size("context"), lax.axis_size("channel")
    rounds = 1
    while 1 << rounds < n_ctx:
        rounds += 1
    operands = (first_stream, value_stream, short_gate, out_gate, mr_filter, li_residue, li_rate, li_skip[None, :], fs, gs, fsh, flh, fl, gl)
    vmem, dma = pltpu.VMEM, pltpu.SemaphoreType.DMA
    shape = jax.ShapeDtypeStruct
    long_out, power = pl.pallas_call(
        functools.partial(fused_kernel, n_ctx, n_chan, chunk),
        in_specs=[pl.BlockSpec(memory_space=pltpu.HBM)] * len(operands),
        out_specs=[pl.BlockSpec(memory_space=pltpu.VMEM)] * 2,
        out_shape=[shape((rows, width), BF16), shape((SUB, rows), F32)],
        scratch_shapes=[vmem(a.shape, a.dtype) for a in operands]
        + [
            vmem((short_n, width), BF16),
            vmem((short_n, width), F32),
            vmem((long_n, width), F32),
            vmem((rows, chunk), F32),
            vmem((rows, width), BF16),
            vmem((rows, width), F32),
            vmem((rows, LANES), F32),
            vmem((poles, width), F32),
            vmem((rounds, poles, width), BF16),
            vmem((rounds + 1, poles, width), BF16),
            vmem((poles, width), F32),
            vmem((rows, LANES), F32),
            vmem((SUB, rows), F32),
            vmem((n_chan - 1, SUB, rows), F32),
            vmem((poles, width), F32),
            vmem((poles, width), F32),
            vmem((poles, SUB, width), F32),
            dma((len(operands) + 2,)),
            dma((chunks,)),
            dma((chunks,)),
            dma((2, rounds + 1)),
            dma((2, rounds + 1)),
            dma((n_chan - 1,)),
            dma((n_chan - 1,)),
        ],
        compiler_params=pltpu.CompilerParams(
            collective_id=0, has_side_effects=True, vmem_limit_bytes=56 * 1024 * 1024
        ),
        cost_estimate=pl.CostEstimate(flops=int(8e9), bytes_accessed=int(8e6), transcendentals=0),
        name="filters",
    )(*operands)
    scale = lax.rsqrt(power[0] / channels + 1e-06)
    gated = out_gate.astype(F32) * long_out.astype(F32)
    return (gated * scale[:, None] * norm_gain[None, :]).astype(BF16)


def solution(mesh):
    both, columns, channel = P("context", "channel"), P(None, "channel"), P("channel")

    def whole_arrays(*args):
        body = functools.partial(on_device, args[0].shape[1])
        return jax.shard_map(
            body,
            mesh=mesh,
            in_specs=(both,) * 4 + (columns,) * 3 + (channel,) * 2,
            out_specs=both,
            check_vma=False,
        )(*args)

    return whole_arrays
```

```python
import functools

import jax
import jax.numpy as jnp
import numpy as np
from jax import lax
from jax.experimental import pallas as pl
from jax.experimental.pallas import tpu as pltpu
from jax.sharding import PartitionSpec as P

F32 = jnp.float32
BF16 = jnp.bfloat16
LANES = 128
SUB = 8


def split_const(a):
    hi = a.astype(BF16)
    lo = (a - hi.astype(np.float64)).astype(BF16)
    return hi, lo


def transforms(block):
    points = 2 * block
    order = np.concatenate([np.arange(0, block, 2), np.arange(1, block, 2)])
    phase = 2.0 * np.pi / points * (order + 0.5)[:, None] * np.arange(points)[None, :]
    full = np.concatenate([np.cos(phase), np.sin(phase)], 0)
    hi, lo = split_const(full[:, :block])
    back = (full.T * (2.0 / points)).astype(BF16)
    return np.concatenate([hi, lo, hi], 1), back[:block], back[block:]


def plus_later(x, later):
    q = x.shape[0] // 4
    a, b, c, d = (x[i * q : (i + 1) * q] for i in range(4))
    e, f, g, h = (later[i * q : (i + 1) * q] for i in range(4))
    return jnp.concatenate([a - g, b + h, c + e, d - f], 0)


def twice(v):
    v = v.astype(BF16)
    return jnp.concatenate([v, v], 0)


def dot(a, b):
    return lax.dot_general(a, b, (((1,), (0,)), ((), ())), preferred_element_type=F32)


def three(v):
    hi = v.astype(BF16)
    lo = (v - hi.astype(F32)).astype(BF16)
    return jnp.concatenate([hi, hi, lo], 0)


def times_spectrum(x, h):
    half = x.shape[0] // 2
    xc, xs, hc, hs = x[:half], x[half:], h[:half], h[half:]
    return jnp.concatenate([xc * hc - xs * hs, xc * hs + xs * hc], 0)


def sublane_index():
    return lax.broadcasted_iota(jnp.int32, (SUB, LANES), 0).astype(F32)


def mode_sums(start, step, blocks, put):
    for a in range(blocks):
        total = start[0]
        for v in start[1:]:
            total = total + v
        put(a, total)
        if a + 1 < blocks:
            start = [v * e for v, e in zip(start, step)]


def rows_of(ref, lanes):
    return [ref[r : r + 1, lanes] for r in range(ref.shape[0])]


MESH = pl.DeviceIdType.MESH


def fused_kernel(n_ctx, n_chan, chunk, *refs):
    n_in = 11
    (first_h, value_h, gate_h, og_h, filt_h, res_h, rate_h, skip_h, fwd_h, back0_h, back1_h) = refs[:n_in]
    long_out, power_out = refs[n_in : n_in + 2]
    (first, value, gate, og, filt, res, rate, skip, fwd, back0, back1) = refs[n_in + 2 : 2 * n_in + 2]
    (x, hs, hl, impulse, mixed, base, total, end, sent, got, state, power, pow_row, pow_got, amp, step8, fade) = refs[
        2 * n_in + 2 : 2 * n_in + 19
    ]
    in_sem, halo_send, halo_recv, st_send, st_recv, pow_send, pow_recv = refs[2 * n_in + 19 :]

    rows, width = first.shape
    taps = filt.shape[0]
    chunks = width // chunk
    here, lane_group = lax.axis_index("context"), lax.axis_index("channel")
    head, tail = pl.ds(0, rows - taps), pl.ds(rows - taps, taps)

    pairs = [
        (first_h.at[tail], first.at[tail]),
        (value_h.at[tail], value.at[tail]),
        (res_h, res),
        (rate_h, rate),
        (filt_h, filt),
        (fwd_h, fwd),
        (first_h.at[head], first.at[head]),
        (value_h.at[head], value.at[head]),
        (back1_h, back1),
        (gate_h, gate),
        (skip_h, skip),
        (back0_h, back0),
        (og_h, og),
    ]
    loads = [pltpu.make_async_copy(a, b, in_sem.at[i]) for i, (a, b) in enumerate(pairs)]
    for load in loads:
        load.start()

    spans = []
    while 2 << len(spans) < n_ctx:
        spans.append(2 << len(spans))
    offsets = sorted({k % n_ctx for s in [1, 2] + spans for k in (s, -s)} - {0})
    barrier = pltpu.get_barrier_semaphore()
    for k in offsets:
        pl.semaphore_signal(barrier, inc=1, device_id={"context": lax.rem(here + k, n_ctx)}, device_id_type=MESH)
    for k in range(1, n_chan):
        pl.semaphore_signal(barrier, inc=1, device_id={"channel": lax.rem(lane_group + k, n_chan)}, device_id_type=MESH)
    loads[0].wait()
    loads[1].wait()
    pl.semaphore_wait(barrier, len(offsets) + n_chan - 1)

    def at_chunk(c):
        return pl.ds(pl.multiple_of(c * chunk, chunk), chunk)

    def product(part, cols):
        return (first[part, cols].astype(F32) * value[part, cols].astype(F32)).astype(BF16)

    def halo_copy(c):
        cols = at_chunk(c)
        return pltpu.make_async_remote_copy(
            src_ref=x.at[pl.ds(rows, taps), cols],
            dst_ref=x.at[pl.ds(0, taps), cols],
            send_sem=halo_send.at[c],
            recv_sem=halo_recv.at[c],
            device_id={"context": lax.rem(here + 1, n_ctx)},
            device_id_type=MESH,
        )

    @pl.loop(0, chunks)
    def _(c):
        cols = at_chunk(c)
        x[pl.ds(rows, taps), cols] = product(tail, cols)
        halo_copy(c).start()

    for load in loads[2:6]:
        load.wait()
    amp[...] = res[...] * jnp.sqrt(2.0 * rate[...])
    step8[...] = jnp.exp(-SUB * rate[...])

    sub = sublane_index()
    poles = rate.shape[0]
    half = chunks // 2

    def lane_tiles(c):
        return [pl.ds(pl.multiple_of(c * chunk + t, LANES), LANES) for t in range(0, chunk, LANES)]

    def steps(lanes):
        return [jnp.broadcast_to(step8[r : r + 1, lanes], (SUB, LANES)) for r in range(poles)]

    def present(k):
        return jnp.where(here >= k, 1.0, 0.0).astype(F32)

    def spectra(c):
        cols = at_chunk(c)
        for t, lanes in enumerate(lane_tiles(c)):
            start = []
            for r in range(poles):
                fading = jnp.exp(-rate[r : r + 1, lanes] * sub)
                fade[r, :, lanes] = fading
                start.append(amp[r : r + 1, lanes] * fading)

            def put(a, v):
                impulse[a * SUB : (a + 1) * SUB, t * LANES : (t + 1) * LANES] = v

            mode_sums(start, steps(lanes), rows // SUB, put)
        hs[:, cols] = dot(fwd[...], three(filt[:, cols]))
        early_h = dot(fwd[:, : 2 * taps], twice(impulse[:taps]))
        hl[: 2 * taps, cols] = early_h
        hl[2 * taps :, cols] = plus_later(early_h, dot(fwd[:, : 2 * taps], twice(impulse[taps:])))

    def short(c):
        cols = at_chunk(c)
        halo_copy(c).wait_recv()
        before = (x[pl.ds(0, taps), cols].astype(F32) * present(1)).astype(BF16)
        parts = [before, product(head, cols), x[pl.ds(rows, taps), cols]]
        parts = [dot(fwd[:, : 2 * taps], twice(p)) for p in parts]
        h = hs[:, cols]
        for i in range(2):
            y = times_spectrum(plus_later(parts[i], parts[i + 1]), h)
            out = dot(back1[...], y.astype(BF16))
            span = pl.ds(i * taps, taps)
            mixed[span, cols] = (gate[span, cols].astype(F32) * out).astype(BF16)

    def ends(c):
        for lanes in lane_tiles(c):
            step = steps(lanes)
            sums = None
            for a in range(0, rows, 16):
                both = mixed[a : a + 16, lanes].astype(F32)
                for part in (both[:SUB], both[SUB:]):
                    sums = [part] * poles if sums is None else [s * e + part for s, e in zip(sums, step)]
            for r, s in enumerate(sums):
                fading = jnp.exp(-rate[r : r + 1, lanes] * (SUB - 1.0 - sub))
                end[r : r + 1, lanes] = jnp.sum(s * fading, axis=0, keepdims=True)

    def local_long(c):
        cols = at_chunk(c)
        x0, x1 = mixed[:taps, cols], mixed[taps:, cols]
        y0, y1 = dot(fwd[:, : 2 * taps], twice(x0)), dot(fwd[:, : 2 * taps], twice(x1))
        h0, h1 = hl[: 2 * taps, cols], hl[2 * taps :, cols]
        later = times_spectrum(y0, h1) + times_spectrum(plus_later(jnp.zeros_like(y1), y1), h0)
        gain = skip[:, cols]
        base[:taps, cols] = dot(back0[...], times_spectrum(y0, h0).astype(BF16)) + gain * x0.astype(F32)
        base[taps:, cols] = dot(back1[...], later.astype(BF16)) + gain * x1.astype(F32)

    def carry(c):
        for lanes in lane_tiles(c):
            start = [state[r : r + 1, lanes] * fade[r, :, lanes] for r in range(poles)]

            def put(a, v):
                total[a * SUB : (a + 1) * SUB, :] = v

            mode_sums(start, steps(lanes), rows // SUB, put)
            out = (base[:, lanes] + total[...]).astype(BF16)
            long_out[:, lanes] = out
            gated = og[:, lanes].astype(F32) * out.astype(F32)
            power[...] += gated * gated

    def scan(part):
        cols = pl.ds(part * half * chunk, half * chunk)

        def state_copy(slot, source, k):
            return pltpu.make_async_remote_copy(
                src_ref=sent.at[source, :, cols],
                dst_ref=got.at[slot, :, cols],
                send_sem=st_send.at[part, slot],
                recv_sem=st_recv.at[part, slot],
                device_id={"context": lax.rem(here + k, n_ctx)},
                device_id_type=MESH,
            )

        rates = rate[:, cols]
        sent[0, :, cols] = end[:, cols].astype(BF16)
        copies = [state_copy(0, 0, 1), state_copy(1, 0, 2)]
        for copy in copies:
            copy.start()
        yield
        for copy in copies:
            copy.wait_recv()
        now = got[0, :, cols].astype(F32) * present(1)
        now = now + jnp.exp(-rates * rows) * (got[1, :, cols].astype(F32) * present(2))
        for i, span in enumerate(spans):
            state[:, cols] = now
            sent[i + 1, :, cols] = now.astype(BF16)
            copy = state_copy(i + 2, i + 1, span)
            copy.start()
            copies.append(copy)
            yield
            copy.wait_recv()
            now = state[:, cols] + jnp.exp(-rates * (rows * span)) * (got[i + 2, :, cols].astype(F32) * present(span))
        state[:, cols] = now * amp[:, cols] * jnp.exp(-rates)
        for copy in copies:
            copy.wait_send()

    def run(body, first_chunk, last_chunk):
        if first_chunk < last_chunk:
            pl.loop(first_chunk, last_chunk)(body)

    def filter_and_next(c):
        short(c)
        spectra(c + 1)
        ends(c)

    spectra(0)
    for load in loads[6:10]:
        load.wait()
    run(filter_and_next, 0, half)
    early, late = scan(0), scan(1)
    next(early, None)
    run(filter_and_next, half, chunks - 1)
    next(early, None)
    short(chunks - 1)
    ends(chunks - 1)
    next(late, None)
    for load in loads[10:]:
        load.wait()
    run(local_long, 0, half)
    next(early, None)
    next(late, None)
    run(local_long, half, chunks)
    for _ in early:
        pass
    next(late, None)
    power[...] = jnp.zeros_like(power)
    run(carry, 0, half)
    for _ in late:
        pass
    run(carry, half, chunks)

    pow_row[...] = lax.dot_general(
        jnp.ones((SUB, LANES), F32),
        power[...],
        (((1,), (1,)), ((), ())),
        precision=lax.Precision.HIGHEST,
        preferred_element_type=F32,
    )
    shares = [
        pltpu.make_async_remote_copy(
            src_ref=pow_row,
            dst_ref=pow_got.at[k - 1],
            send_sem=pow_send.at[k - 1],
            recv_sem=pow_recv.at[k - 1],
            device_id={"channel": lax.rem(lane_group + k, n_chan)},
            device_id_type=MESH,
        )
        for k in range(1, n_chan)
    ]
    for copy in shares:
        copy.start()

    @pl.loop(0, chunks)
    def _(c):
        halo_copy(c).wait_send()

    for copy in shares:
        copy.wait()
    whole = pow_row[...]
    for k in range(n_chan - 1):
        whole = whole + pow_got[k]
    power_out[...] = whole


def on_device(channels, first_stream, value_stream, short_gate, out_gate, mr_filter, li_residue, li_rate, li_skip, norm_gain):
    rows, width = first_stream.shape
    taps, poles = mr_filter.shape[0], li_residue.shape[0]
    chunk = min(512, width // 2)
    chunks = width // chunk
    short_n, long_n = rows + taps, 2 * rows
    assert rows == 2 * taps
    fwd, back0, back1 = transforms(taps)
    n_ctx, n_chan = lax.axis_size("context"), lax.axis_size("channel")
    rounds = 1
    while 1 << rounds < n_ctx:
        rounds += 1
    operands = (first_stream, value_stream, short_gate, out_gate, mr_filter, li_residue, li_rate, li_skip[None, :], fwd, back0, back1)
    vmem, dma = pltpu.VMEM, pltpu.SemaphoreType.DMA
    shape = jax.ShapeDtypeStruct
    long_out, power = pl.pallas_call(
        functools.partial(fused_kernel, n_ctx, n_chan, chunk),
        in_specs=[pl.BlockSpec(memory_space=pltpu.HBM)] * len(operands),
        out_specs=[pl.BlockSpec(memory_space=pltpu.VMEM)] * 2,
        out_shape=[shape((rows, width), BF16), shape((SUB, rows), F32)],
        scratch_shapes=[vmem(a.shape, a.dtype) for a in operands]
        + [
            vmem((short_n, width), BF16),
            vmem((rows, width), F32),
            vmem((long_n, width), F32),
            vmem((rows, chunk), F32),
            vmem((rows, width), BF16),
            vmem((rows, width), F32),
            vmem((rows, LANES), F32),
            vmem((poles, width), F32),
            vmem((rounds, poles, width), BF16),
            vmem((rounds + 1, poles, width), BF16),
            vmem((poles, width), F32),
            vmem((rows, LANES), F32),
            vmem((SUB, rows), F32),
            vmem((n_chan - 1, SUB, rows), F32),
            vmem((poles, width), F32),
            vmem((poles, width), F32),
            vmem((poles, SUB, width), F32),
            dma((len(operands) + 2,)),
            dma((chunks,)),
            dma((chunks,)),
            dma((2, rounds + 1)),
            dma((2, rounds + 1)),
            dma((n_chan - 1,)),
            dma((n_chan - 1,)),
        ],
        compiler_params=pltpu.CompilerParams(
            collective_id=0, has_side_effects=True, vmem_limit_bytes=40 * 1024 * 1024
        ),
        cost_estimate=pl.CostEstimate(flops=int(8e9), bytes_accessed=int(8e6), transcendentals=0),
        name="filters",
    )(*operands)
    scale = lax.rsqrt(power[0] / channels + 1e-06)
    gated = out_gate.astype(F32) * long_out.astype(F32)
    return (gated * scale[:, None] * norm_gain[None, :]).astype(BF16)


def solution(mesh):
    both, columns, channel = P("context", "channel"), P(None, "channel"), P("channel")

    def whole_arrays(*args):
        body = functools.partial(on_device, args[0].shape[1])
        return jax.shard_map(
            body,
            mesh=mesh,
            in_specs=(both,) * 4 + (columns,) * 3 + (channel,) * 2,
            out_specs=both,
            check_vma=False,
        )(*args)

    return whole_arrays
```

```python
import functools

import jax
import jax.numpy as jnp
import numpy as np
from jax import lax
from jax.experimental import pallas as pl
from jax.experimental.pallas import tpu as pltpu
from jax.sharding import PartitionSpec as P

F32 = jnp.float32
BF16 = jnp.bfloat16
LANES = 128
SUB = 8


def split_const(a):
    hi = a.astype(BF16)
    lo = (a - hi.astype(np.float64)).astype(BF16)
    return hi, lo


def transforms(block):
    points = 2 * block
    order = np.concatenate([np.arange(0, block, 2), np.arange(1, block, 2)])
    phase = 2.0 * np.pi / points * (order + 0.5)[:, None] * np.arange(points)[None, :]
    full = np.concatenate([np.cos(phase), np.sin(phase)], 0)
    hi, lo = split_const(full[:, :block])
    back = (full.T * (2.0 / points)).astype(BF16)
    return np.concatenate([hi, lo, hi], 1), back[:block], back[block:]


def plus_later(x, later):
    q = x.shape[0] // 4
    a, b, c, d = (x[i * q : (i + 1) * q] for i in range(4))
    e, f, g, h = (later[i * q : (i + 1) * q] for i in range(4))
    return jnp.concatenate([a - g, b + h, c + e, d - f], 0)


def twice(v):
    v = v.astype(BF16)
    return jnp.concatenate([v, v], 0)


def dot(a, b):
    return lax.dot_general(a, b, (((1,), (0,)), ((), ())), preferred_element_type=F32)


def three(v):
    hi = v.astype(BF16)
    lo = (v - hi.astype(F32)).astype(BF16)
    return jnp.concatenate([hi, hi, lo], 0)


def times_spectrum(x, h):
    half = x.shape[0] // 2
    xc, xs, hc, hs = x[:half], x[half:], h[:half], h[half:]
    return jnp.concatenate([xc * hc - xs * hs, xc * hs + xs * hc], 0)


def sublane_index():
    return lax.broadcasted_iota(jnp.int32, (SUB, LANES), 0).astype(F32)


def mode_sums(start, step, blocks, put):
    for a in range(blocks):
        total = start[0]
        for v in start[1:]:
            total = total + v
        put(a, total)
        if a + 1 < blocks:
            start = [v * e for v, e in zip(start, step)]


def rows_of(ref, lanes):
    return [ref[r : r + 1, lanes] for r in range(ref.shape[0])]


MESH = pl.DeviceIdType.MESH


def scan_plan(count):
    plan, window = [[1, 2]], 2
    while window < count:
        plan.append([k * window for k in (1, 2, 3) if k * window < count])
        window *= 4
    return plan


def fused_kernel(n_ctx, n_chan, chunk, *refs):
    n_in = 11
    (first_h, value_h, gate_h, og_h, filt_h, res_h, rate_h, skip_h, fwd_h, back0_h, back1_h) = refs[:n_in]
    long_out, power_out = refs[n_in : n_in + 2]
    (first, value, gate, og, filt, res, rate, skip, fwd, back0, back1) = refs[n_in + 2 : 2 * n_in + 2]
    (x, hs, hl, impulse, mixed, base, total, end, sent, got, state, power, pow_row, pow_got, amp, step8, fade, out_buf) = refs[
        2 * n_in + 2 : 2 * n_in + 20
    ]
    in_sem, halo_send, halo_recv, st_send, st_recv, pow_send, pow_recv, out_sem = refs[2 * n_in + 20 :]

    rows, width = first.shape
    taps = filt.shape[0]
    chunks = width // chunk
    here, lane_group = lax.axis_index("context"), lax.axis_index("channel")
    head, tail = pl.ds(0, rows - taps), pl.ds(rows - taps, taps)

    pairs = [
        (first_h.at[tail], first.at[tail]),
        (value_h.at[tail], value.at[tail]),
        (res_h, res),
        (rate_h, rate),
        (filt_h, filt),
        (fwd_h, fwd),
        (first_h.at[head], first.at[head]),
        (value_h.at[head], value.at[head]),
        (back1_h, back1),
        (gate_h, gate),
        (skip_h, skip),
        (back0_h, back0),
        (og_h, og),
    ]
    loads = [pltpu.make_async_copy(a, b, in_sem.at[i]) for i, (a, b) in enumerate(pairs)]
    for load in loads[:2]:
        load.start()

    plan = scan_plan(n_ctx)
    offsets = sorted({k % n_ctx for shifts in plan for s in shifts for k in (s, -s)} - {0})
    barrier = pltpu.get_barrier_semaphore()
    for k in offsets:
        pl.semaphore_signal(barrier, inc=1, device_id={"context": lax.rem(here + k, n_ctx)}, device_id_type=MESH)
    for k in range(1, n_chan):
        pl.semaphore_signal(barrier, inc=1, device_id={"channel": lax.rem(lane_group + k, n_chan)}, device_id_type=MESH)
    loads[0].wait()
    loads[1].wait()
    for load in loads[2:]:
        load.start()
    pl.semaphore_wait(barrier, len(offsets) + n_chan - 1)

    def at_chunk(c):
        return pl.ds(pl.multiple_of(c * chunk, chunk), chunk)

    def product(part, cols):
        return (first[part, cols].astype(F32) * value[part, cols].astype(F32)).astype(BF16)

    def halo_copy(c):
        cols = at_chunk(c)
        return pltpu.make_async_remote_copy(
            src_ref=x.at[pl.ds(rows, taps), cols],
            dst_ref=x.at[pl.ds(0, taps), cols],
            send_sem=halo_send.at[c],
            recv_sem=halo_recv.at[c],
            device_id={"context": lax.rem(here + 1, n_ctx)},
            device_id_type=MESH,
        )

    @pl.loop(0, chunks)
    def _(c):
        cols = at_chunk(c)
        x[pl.ds(rows, taps), cols] = product(tail, cols)
        halo_copy(c).start()

    for load in loads[2:6]:
        load.wait()
    amp[...] = res[...] * jnp.sqrt(2.0 * rate[...])
    step8[...] = jnp.exp(-SUB * rate[...])

    sub = sublane_index()
    poles = rate.shape[0]
    half = chunks - 1

    def lane_tiles(c):
        return [pl.ds(pl.multiple_of(c * chunk + t, LANES), LANES) for t in range(0, chunk, LANES)]

    def steps(lanes):
        return [jnp.broadcast_to(step8[r : r + 1, lanes], (SUB, LANES)) for r in range(poles)]

    def present(k):
        return jnp.where(here >= k, 1.0, 0.0).astype(F32)

    def spectra(c):
        cols = at_chunk(c)
        for t, lanes in enumerate(lane_tiles(c)):
            start = []
            for r in range(poles):
                fading = jnp.exp(-rate[r : r + 1, lanes] * sub)
                fade[r, :, lanes] = fading
                start.append(amp[r : r + 1, lanes] * fading)

            def put(a, v):
                impulse[a * SUB : (a + 1) * SUB, t * LANES : (t + 1) * LANES] = v

            mode_sums(start, steps(lanes), rows // SUB, put)
        hs[:, cols] = dot(fwd[...], three(filt[:, cols]))
        early_h = dot(fwd[:, : 2 * taps], twice(impulse[:taps]))
        hl[: 2 * taps, cols] = early_h
        hl[2 * taps :, cols] = plus_later(early_h, dot(fwd[:, : 2 * taps], twice(impulse[taps:])))

    def short(c):
        cols = at_chunk(c)
        halo_copy(c).wait_recv()
        before = (x[pl.ds(0, taps), cols].astype(F32) * present(1)).astype(BF16)
        parts = [before, product(head, cols), x[pl.ds(rows, taps), cols]]
        parts = [dot(fwd[:, : 2 * taps], twice(p)) for p in parts]
        h = hs[:, cols]
        for i in range(2):
            y = times_spectrum(plus_later(parts[i], parts[i + 1]), h)
            out = dot(back1[...], y.astype(BF16))
            span = pl.ds(i * taps, taps)
            mixed[span, cols] = (gate[span, cols].astype(F32) * out).astype(BF16)

    def ends(c):
        for lanes in lane_tiles(c):
            step = steps(lanes)
            sums = None
            for a in range(0, rows, 16):
                both = mixed[a : a + 16, lanes].astype(F32)
                for part in (both[:SUB], both[SUB:]):
                    sums = [part] * poles if sums is None else [s * e + part for s, e in zip(sums, step)]
            for r, s in enumerate(sums):
                fading = jnp.exp(-rate[r : r + 1, lanes] * (SUB - 1.0 - sub))
                end[r : r + 1, lanes] = jnp.sum(s * fading, axis=0, keepdims=True)

    def local_long(c):
        cols = at_chunk(c)
        x0, x1 = mixed[:taps, cols], mixed[taps:, cols]
        y0, y1 = dot(fwd[:, : 2 * taps], twice(x0)), dot(fwd[:, : 2 * taps], twice(x1))
        h0, h1 = hl[: 2 * taps, cols], hl[2 * taps :, cols]
        later = times_spectrum(y0, h1) + times_spectrum(plus_later(jnp.zeros_like(y1), y1), h0)
        gain = skip[:, cols]
        base[:taps, cols] = dot(back0[...], times_spectrum(y0, h0).astype(BF16)) + gain * x0.astype(F32)
        base[taps:, cols] = dot(back1[...], later.astype(BF16)) + gain * x1.astype(F32)

    def carry(c):
        for lanes in lane_tiles(c):
            start = [state[r : r + 1, lanes] * fade[r, :, lanes] for r in range(poles)]

            def put(a, v):
                total[a * SUB : (a + 1) * SUB, :] = v

            mode_sums(start, steps(lanes), rows // SUB, put)
            out = (base[:, lanes] + total[...]).astype(BF16)
            out_buf[:, lanes] = out
            gated = og[:, lanes].astype(F32) * out.astype(F32)
            power[...] += gated * gated

    def scan(part):
        cols = pl.ds(part * half * chunk, (chunks - half if part else half) * chunk)
        rates = rate[:, cols]
        now, copies, slot = end[:, cols], [], 0
        for i, shifts in enumerate(plan):
            sent[i, :, cols] = now.astype(BF16)
            state[:, cols] = now
            for j, k in enumerate(shifts):
                copy = pltpu.make_async_remote_copy(
                    src_ref=sent.at[i, :, cols],
                    dst_ref=got.at[slot + j, :, cols],
                    send_sem=st_send.at[part, slot + j],
                    recv_sem=st_recv.at[part, slot + j],
                    device_id={"context": lax.rem(here + k, n_ctx)},
                    device_id_type=MESH,
                )
                copy.start()
                copies.append(copy)
            yield
            now = state[:, cols] if i else jnp.zeros_like(rates)
            for j, k in enumerate(shifts):
                copies[slot + j].wait_recv()
                faded = jnp.exp(-rates * (rows * (k if i else k - 1)))
                now = now + faded * (got[slot + j, :, cols].astype(F32) * present(k))
            slot += len(shifts)
        state[:, cols] = now * amp[:, cols] * jnp.exp(-rates)
        for copy in copies:
            copy.wait_send()

    def write_back(part):
        cols = pl.ds(part * half * chunk, (chunks - half if part else half) * chunk)
        return pltpu.make_async_copy(out_buf.at[:, cols], long_out.at[:, cols], out_sem.at[part])

    def run(body, first_chunk, last_chunk):
        if first_chunk < last_chunk:
            pl.loop(first_chunk, last_chunk)(body)

    def filter_and_next(c):
        short(c)
        spectra(c + 1)
        ends(c)

    spectra(0)
    for load in loads[6:10]:
        load.wait()
    run(filter_and_next, 0, half)
    early, late = scan(0), scan(1)
    next(early, None)
    short(chunks - 1)
    ends(chunks - 1)
    next(late, None)
    next(early, None)
    for load in loads[10:]:
        load.wait()
    run(local_long, 0, half)
    next(late, None)
    run(local_long, half, chunks)
    for _ in early:
        pass
    power[...] = jnp.zeros_like(power)
    run(carry, 0, half)
    write_back(0).start()
    for _ in late:
        pass
    run(carry, half, chunks)
    write_back(1).start()

    pow_row[...] = lax.dot_general(
        jnp.ones((SUB, LANES), F32),
        power[...],
        (((1,), (1,)), ((), ())),
        precision=lax.Precision.HIGHEST,
        preferred_element_type=F32,
    )
    shares = [
        pltpu.make_async_remote_copy(
            src_ref=pow_row,
            dst_ref=pow_got.at[k - 1],
            send_sem=pow_send.at[k - 1],
            recv_sem=pow_recv.at[k - 1],
            device_id={"channel": lax.rem(lane_group + k, n_chan)},
            device_id_type=MESH,
        )
        for k in range(1, n_chan)
    ]
    for copy in shares:
        copy.start()

    @pl.loop(0, chunks)
    def _(c):
        halo_copy(c).wait_send()

    for copy in shares:
        copy.wait()
    whole = pow_row[...]
    for k in range(n_chan - 1):
        whole = whole + pow_got[k]
    power_out[...] = whole
    write_back(0).wait()
    write_back(1).wait()


def on_device(channels, first_stream, value_stream, short_gate, out_gate, mr_filter, li_residue, li_rate, li_skip, norm_gain):
    rows, width = first_stream.shape
    taps, poles = mr_filter.shape[0], li_residue.shape[0]
    chunk = min(512, width // 2)
    chunks = width // chunk
    short_n, long_n = rows + taps, 2 * rows
    assert rows == 2 * taps
    fwd, back0, back1 = transforms(taps)
    n_ctx, n_chan = lax.axis_size("context"), lax.axis_size("channel")
    plan = scan_plan(n_ctx)
    rounds, slots = len(plan), sum(len(shifts) for shifts in plan)
    operands = (first_stream, value_stream, short_gate, out_gate, mr_filter, li_residue, li_rate, li_skip[None, :], fwd, back0, back1)
    vmem, dma = pltpu.VMEM, pltpu.SemaphoreType.DMA
    shape = jax.ShapeDtypeStruct
    long_out, power = pl.pallas_call(
        functools.partial(fused_kernel, n_ctx, n_chan, chunk),
        in_specs=[pl.BlockSpec(memory_space=pltpu.HBM)] * len(operands),
        out_specs=[pl.BlockSpec(memory_space=pltpu.HBM), pl.BlockSpec(memory_space=pltpu.VMEM)],
        out_shape=[shape((rows, width), BF16), shape((SUB, rows), F32)],
        scratch_shapes=[vmem(a.shape, a.dtype) for a in operands]
        + [
            vmem((short_n, width), BF16),
            vmem((rows, width), F32),
            vmem((long_n, width), F32),
            vmem((rows, chunk), F32),
            vmem((rows, width), BF16),
            vmem((rows, width), F32),
            vmem((rows, LANES), F32),
            vmem((poles, width), F32),
            vmem((rounds, poles, width), BF16),
            vmem((slots, poles, width), BF16),
            vmem((poles, width), F32),
            vmem((rows, LANES), F32),
            vmem((SUB, rows), F32),
            vmem((n_chan - 1, SUB, rows), F32),
            vmem((poles, width), F32),
            vmem((poles, width), F32),
            vmem((poles, SUB, width), F32),
            vmem((rows, width), BF16),
            dma((len(operands) + 2,)),
            dma((chunks,)),
            dma((chunks,)),
            dma((2, slots)),
            dma((2, slots)),
            dma((n_chan - 1,)),
            dma((n_chan - 1,)),
            dma((2,)),
        ],
        compiler_params=pltpu.CompilerParams(
            collective_id=0, has_side_effects=True, vmem_limit_bytes=56 * 1024 * 1024
        ),
        cost_estimate=pl.CostEstimate(flops=int(8e9), bytes_accessed=int(8e6), transcendentals=0),
        name="filters",
    )(*operands)
    scale = lax.rsqrt(power[0] / channels + 1e-06)
    gated = out_gate.astype(F32) * long_out.astype(F32)
    return (gated * scale[:, None] * norm_gain[None, :]).astype(BF16)


def solution(mesh):
    both, columns, channel = P("context", "channel"), P(None, "channel"), P("channel")

    def whole_arrays(*args):
        body = functools.partial(on_device, args[0].shape[1])
        return jax.shard_map(
            body,
            mesh=mesh,
            in_specs=(both,) * 4 + (columns,) * 3 + (channel,) * 2,
            out_specs=both,
            check_vma=False,
        )(*args)

    return whole_arrays
```

```python
import functools

import jax
import jax.numpy as jnp
import numpy as np
from jax import lax
from jax.experimental import pallas as pl
from jax.experimental.pallas import tpu as pltpu
from jax.sharding import PartitionSpec as P

F32 = jnp.float32
BF16 = jnp.bfloat16
LANES = 128
SUB = 8


def split_const(a):
    hi = a.astype(BF16)
    lo = (a - hi.astype(np.float64)).astype(BF16)
    return hi, lo


def transforms(block):
    points = 2 * block
    order = np.concatenate([np.arange(0, block, 2), np.arange(1, block, 2)])
    phase = 2.0 * np.pi / points * (order + 0.5)[:, None] * np.arange(points)[None, :]
    full = np.concatenate([np.cos(phase), np.sin(phase)], 0)
    hi, lo = split_const(full[:, :block])
    back = (full.T * (2.0 / points)).astype(BF16)
    return np.concatenate([hi, lo, hi], 1), back[:block], back[block:]


def plus_later(x, later):
    q = x.shape[0] // 4
    a, b, c, d = (x[i * q : (i + 1) * q] for i in range(4))
    e, f, g, h = (later[i * q : (i + 1) * q] for i in range(4))
    return jnp.concatenate([a - g, b + h, c + e, d - f], 0)


def twice(v):
    v = v.astype(BF16)
    return jnp.concatenate([v, v], 0)


def dot(a, b):
    return lax.dot_general(a, b, (((1,), (0,)), ((), ())), preferred_element_type=F32)


def three(v):
    hi = v.astype(BF16)
    lo = (v - hi.astype(F32)).astype(BF16)
    return jnp.concatenate([hi, hi, lo], 0)


def times_spectrum(x, h):
    half = x.shape[0] // 2
    xc, xs, hc, hs = x[:half], x[half:], h[:half], h[half:]
    return jnp.concatenate([xc * hc - xs * hs, xc * hs + xs * hc], 0)


def sublane_index():
    return lax.broadcasted_iota(jnp.int32, (SUB, LANES), 0).astype(F32)


def mode_sums(start, step, blocks, put):
    for a in range(blocks):
        total = start[0]
        for v in start[1:]:
            total = total + v
        put(a, total)
        if a + 1 < blocks:
            start = [v * e for v, e in zip(start, step)]


def rows_of(ref, lanes):
    return [ref[r : r + 1, lanes] for r in range(ref.shape[0])]


MESH = pl.DeviceIdType.MESH


def scan_plan(count):
    plan, window = [[1, 2]], 2
    while window < count:
        plan.append([k * window for k in (1, 2, 3) if k * window < count])
        window *= 4
    return plan


def fused_kernel(n_ctx, n_chan, chunk, *refs):
    n_in = 11
    (first_h, value_h, gate_h, og_h, filt_h, res_h, rate_h, skip_h, fwd_h, back0_h, back1_h) = refs[:n_in]
    long_out, power_out = refs[n_in : n_in + 2]
    (first, value, gate, og, filt, res, rate, skip, fwd, back0, back1) = refs[n_in + 2 : 2 * n_in + 2]
    (x, hs, hl, impulse, mixed, base, total, end, sent, got, state, power, pow_row, pow_got, amp, step8, fade, out_buf) = refs[
        2 * n_in + 2 : 2 * n_in + 20
    ]
    in_sem, halo_send, halo_recv, st_send, st_recv, pow_send, pow_recv, out_sem = refs[2 * n_in + 20 :]

    rows, width = first.shape
    taps = filt.shape[0]
    chunks = width // chunk
    here, lane_group = lax.axis_index("context"), lax.axis_index("channel")
    head, tail = pl.ds(0, rows - taps), pl.ds(rows - taps, taps)

    pairs = [
        (first_h.at[tail], first.at[tail]),
        (value_h.at[tail], value.at[tail]),
        (res_h, res),
        (rate_h, rate),
        (filt_h, filt),
        (fwd_h, fwd),
        (first_h.at[head], first.at[head]),
        (value_h.at[head], value.at[head]),
        (back1_h, back1),
        (gate_h, gate),
        (skip_h, skip),
        (back0_h, back0),
        (og_h, og),
    ]
    loads = [pltpu.make_async_copy(a, b, in_sem.at[i]) for i, (a, b) in enumerate(pairs)]
    for load in loads[:2]:
        load.start()

    plan = scan_plan(n_ctx)
    offsets = sorted({k % n_ctx for shifts in plan for s in shifts for k in (s, -s)} - {0})
    barrier = pltpu.get_barrier_semaphore()
    for k in offsets:
        pl.semaphore_signal(barrier, inc=1, device_id={"context": lax.rem(here + k, n_ctx)}, device_id_type=MESH)
    for k in range(1, n_chan):
        pl.semaphore_signal(barrier, inc=1, device_id={"channel": lax.rem(lane_group + k, n_chan)}, device_id_type=MESH)
    loads[0].wait()
    loads[1].wait()
    for load in loads[2:]:
        load.start()
    pl.semaphore_wait(barrier, len(offsets) + n_chan - 1)

    def at_chunk(c):
        return pl.ds(pl.multiple_of(c * chunk, chunk), chunk)

    def product(part, cols):
        return (first[part, cols].astype(F32) * value[part, cols].astype(F32)).astype(BF16)

    def halo_copy(c):
        cols = at_chunk(c)
        return pltpu.make_async_remote_copy(
            src_ref=x.at[pl.ds(rows, taps), cols],
            dst_ref=x.at[pl.ds(0, taps), cols],
            send_sem=halo_send.at[c],
            recv_sem=halo_recv.at[c],
            device_id={"context": lax.rem(here + 1, n_ctx)},
            device_id_type=MESH,
        )

    @pl.loop(0, chunks)
    def _(c):
        cols = at_chunk(c)
        x[pl.ds(rows, taps), cols] = product(tail, cols)
        halo_copy(c).start()

    for load in loads[2:6]:
        load.wait()
    amp[...] = res[...] * jnp.sqrt(2.0 * rate[...])
    step8[...] = jnp.exp(-SUB * rate[...])

    sub = sublane_index()
    poles = rate.shape[0]
    half = chunks - 1

    def lane_tiles(c):
        return [pl.ds(pl.multiple_of(c * chunk + t, LANES), LANES) for t in range(0, chunk, LANES)]

    def steps(lanes):
        return [jnp.broadcast_to(step8[r : r + 1, lanes], (SUB, LANES)) for r in range(poles)]

    def present(k):
        return jnp.where(here >= k, 1.0, 0.0).astype(F32)

    def spectra(c):
        cols = at_chunk(c)
        for t, lanes in enumerate(lane_tiles(c)):
            start = []
            for r in range(poles):
                fading = jnp.exp(-rate[r : r + 1, lanes] * sub)
                fade[r, :, lanes] = fading
                start.append(amp[r : r + 1, lanes] * fading)

            def put(a, v):
                impulse[a * SUB : (a + 1) * SUB, t * LANES : (t + 1) * LANES] = v

            mode_sums(start, steps(lanes), rows // SUB, put)
        hs[:, cols] = dot(fwd[...], three(filt[:, cols]))
        early_h = dot(fwd[:, : 2 * taps], twice(impulse[:taps]))
        hl[: 2 * taps, cols] = early_h
        hl[2 * taps :, cols] = plus_later(early_h, dot(fwd[:, : 2 * taps], twice(impulse[taps:])))

    def short(c):
        cols = at_chunk(c)
        halo_copy(c).wait_recv()
        before = (x[pl.ds(0, taps), cols].astype(F32) * present(1)).astype(BF16)
        parts = [before, product(head, cols), x[pl.ds(rows, taps), cols]]
        parts = [dot(fwd[:, : 2 * taps], twice(p)) for p in parts]
        h = hs[:, cols]
        for i in range(2):
            y = times_spectrum(plus_later(parts[i], parts[i + 1]), h)
            out = dot(back1[...], y.astype(BF16))
            span = pl.ds(i * taps, taps)
            mixed[span, cols] = (gate[span, cols].astype(F32) * out).astype(BF16)

    def ends(c):
        for lanes in lane_tiles(c):
            step = steps(lanes)
            sums = None
            for a in range(0, rows, 16):
                both = mixed[a : a + 16, lanes].astype(F32)
                for part in (both[:SUB], both[SUB:]):
                    sums = [part] * poles if sums is None else [s * e + part for s, e in zip(sums, step)]
            for r, s in enumerate(sums):
                fading = jnp.exp(-rate[r : r + 1, lanes] * (SUB - 1.0 - sub))
                end[r : r + 1, lanes] = jnp.sum(s * fading, axis=0, keepdims=True)

    def local_long(c):
        cols = at_chunk(c)
        x0, x1 = mixed[:taps, cols], mixed[taps:, cols]
        y0, y1 = dot(fwd[:, : 2 * taps], twice(x0)), dot(fwd[:, : 2 * taps], twice(x1))
        h0, h1 = hl[: 2 * taps, cols], hl[2 * taps :, cols]
        later = times_spectrum(y0, h1) + times_spectrum(plus_later(jnp.zeros_like(y1), y1), h0)
        gain = skip[:, cols]
        base[:taps, cols] = dot(back0[...], times_spectrum(y0, h0).astype(BF16)) + gain * x0.astype(F32)
        base[taps:, cols] = dot(back1[...], later.astype(BF16)) + gain * x1.astype(F32)

    def carry(c):
        for lanes in lane_tiles(c):
            start = [state[r : r + 1, lanes] * fade[r, :, lanes] for r in range(poles)]

            def put(a, v):
                total[a * SUB : (a + 1) * SUB, :] = v

            mode_sums(start, steps(lanes), rows // SUB, put)
            out = (base[:, lanes] + total[...]).astype(BF16)
            out_buf[:, lanes] = out
            gated = og[:, lanes].astype(F32) * out.astype(F32)
            power[...] += gated * gated

    def scan(part):
        cols = pl.ds(part * half * chunk, (chunks - half if part else half) * chunk)
        rates = rate[:, cols]
        now, copies, slot = end[:, cols], [], 0
        for i, shifts in enumerate(plan):
            sent[i, :, cols] = now.astype(BF16)
            state[:, cols] = now
            for j, k in enumerate(shifts):
                copy = pltpu.make_async_remote_copy(
                    src_ref=sent.at[i, :, cols],
                    dst_ref=got.at[slot + j, :, cols],
                    send_sem=st_send.at[part, slot + j],
                    recv_sem=st_recv.at[part, slot + j],
                    device_id={"context": lax.rem(here + k, n_ctx)},
                    device_id_type=MESH,
                )
                copy.start()
                copies.append(copy)
            yield
            now = state[:, cols] if i else jnp.zeros_like(rates)
            for j, k in enumerate(shifts):
                copies[slot + j].wait_recv()
                faded = jnp.exp(-rates * (rows * (k if i else k - 1)))
                now = now + faded * (got[slot + j, :, cols].astype(F32) * present(k))
            slot += len(shifts)
        state[:, cols] = now * amp[:, cols] * jnp.exp(-rates)
        for copy in copies:
            copy.wait_send()

    def write_back(part):
        cols = pl.ds(part * half * chunk, (chunks - half if part else half) * chunk)
        return pltpu.make_async_copy(out_buf.at[:, cols], long_out.at[:, cols], out_sem.at[part])

    def run(body, first_chunk, last_chunk):
        if first_chunk < last_chunk:
            pl.loop(first_chunk, last_chunk)(body)

    def filter_and_next(c):
        short(c)
        spectra(c + 1)
        ends(c)

    spectra(0)
    for load in loads[6:10]:
        load.wait()
    run(filter_and_next, 0, half)
    early, late = scan(0), scan(1)
    next(early, None)
    short(chunks - 1)
    ends(chunks - 1)
    next(late, None)
    next(early, None)
    for load in loads[10:]:
        load.wait()
    run(local_long, 0, half)
    next(late, None)
    run(local_long, half, chunks)
    for _ in early:
        pass
    power[...] = jnp.zeros_like(power)
    run(carry, 0, half)
    write_back(0).start()
    for _ in late:
        pass
    run(carry, half, chunks)
    write_back(1).start()

    pow_row[...] = lax.dot_general(
        jnp.ones((SUB, LANES), F32),
        power[...],
        (((1,), (1,)), ((), ())),
        precision=lax.Precision.HIGHEST,
        preferred_element_type=F32,
    )
    shares = [
        pltpu.make_async_remote_copy(
            src_ref=pow_row,
            dst_ref=pow_got.at[k - 1],
            send_sem=pow_send.at[k - 1],
            recv_sem=pow_recv.at[k - 1],
            device_id={"channel": lax.rem(lane_group + k, n_chan)},
            device_id_type=MESH,
        )
        for k in range(1, n_chan)
    ]
    for copy in shares:
        copy.start()

    @pl.loop(0, chunks)
    def _(c):
        halo_copy(c).wait_send()

    for copy in shares:
        copy.wait()
    whole = pow_row[...]
    for k in range(n_chan - 1):
        whole = whole + pow_got[k]
    power_out[...] = whole
    write_back(0).wait()
    write_back(1).wait()


def on_device(channels, first_stream, value_stream, short_gate, out_gate, mr_filter, li_residue, li_rate, li_skip, norm_gain):
    rows, width = first_stream.shape
    taps, poles = mr_filter.shape[0], li_residue.shape[0]
    chunk = min(256, width // 2)
    chunks = width // chunk
    short_n, long_n = rows + taps, 2 * rows
    assert rows == 2 * taps
    fwd, back0, back1 = transforms(taps)
    n_ctx, n_chan = lax.axis_size("context"), lax.axis_size("channel")
    plan = scan_plan(n_ctx)
    rounds, slots = len(plan), sum(len(shifts) for shifts in plan)
    operands = (first_stream, value_stream, short_gate, out_gate, mr_filter, li_residue, li_rate, li_skip[None, :], fwd, back0, back1)
    vmem, dma = pltpu.VMEM, pltpu.SemaphoreType.DMA
    shape = jax.ShapeDtypeStruct
    long_out, power = pl.pallas_call(
        functools.partial(fused_kernel, n_ctx, n_chan, chunk),
        in_specs=[pl.BlockSpec(memory_space=pltpu.HBM)] * len(operands),
        out_specs=[pl.BlockSpec(memory_space=pltpu.HBM), pl.BlockSpec(memory_space=pltpu.VMEM)],
        out_shape=[shape((rows, width), BF16), shape((SUB, rows), F32)],
        scratch_shapes=[vmem(a.shape, a.dtype) for a in operands]
        + [
            vmem((short_n, width), BF16),
            vmem((rows, width), F32),
            vmem((long_n, width), F32),
            vmem((rows, chunk), F32),
            vmem((rows, width), BF16),
            vmem((rows, width), F32),
            vmem((rows, LANES), F32),
            vmem((poles, width), F32),
            vmem((rounds, poles, width), BF16),
            vmem((slots, poles, width), BF16),
            vmem((poles, width), F32),
            vmem((rows, LANES), F32),
            vmem((SUB, rows), F32),
            vmem((n_chan - 1, SUB, rows), F32),
            vmem((poles, width), F32),
            vmem((poles, width), F32),
            vmem((poles, SUB, width), F32),
            vmem((rows, width), BF16),
            dma((len(operands) + 2,)),
            dma((chunks,)),
            dma((chunks,)),
            dma((2, slots)),
            dma((2, slots)),
            dma((n_chan - 1,)),
            dma((n_chan - 1,)),
            dma((2,)),
        ],
        compiler_params=pltpu.CompilerParams(
            collective_id=0, has_side_effects=True, vmem_limit_bytes=56 * 1024 * 1024
        ),
        cost_estimate=pl.CostEstimate(flops=int(8e9), bytes_accessed=int(8e6), transcendentals=0),
        name="filters",
    )(*operands)
    scale = lax.rsqrt(power[0] / channels + 1e-06)
    gated = out_gate.astype(F32) * long_out.astype(F32)
    return (gated * scale[:, None] * norm_gain[None, :]).astype(BF16)


def solution(mesh):
    both, columns, channel = P("context", "channel"), P(None, "channel"), P("channel")

    def whole_arrays(*args):
        body = functools.partial(on_device, args[0].shape[1])
        return jax.shard_map(
            body,
            mesh=mesh,
            in_specs=(both,) * 4 + (columns,) * 3 + (channel,) * 2,
            out_specs=both,
            check_vma=False,
        )(*args)

    return whole_arrays
```
